32 devices in a mesh: label: 8 (over z, y), doc: 4 (over x, core).
Axes of the slice: x: 2, y: 2, z: 4, core: 2. Of those that a mesh axis runs over, the one named last changes fastest.
Arguments:
- doc_embed: bfloat16 [512, 768], P(('doc', 'label')), may hold values from -1 to 1
- classifier: bfloat16 [256, 64, 768], P('label'), may hold values from -3 to 3
- shortlist: int32 [4, 8, 32], P('doc', 'label'), may hold values from 0 to 255, as said below
- positives: int32 [512, 8], P('doc'), may hold values from 0 to 16383, as said below
Outputs:
- doc_grad: bfloat16 [512, 768], P(('doc', 'label'))
- class_grad: float32 [256, 64, 768], P(('label', 'doc'))
- mean_loss: float32 [], replicated
The draws below stay inside these ranges and needn't reach their ends.
Inputs may be any that keep to these rules, and one draw needn't show every extreme that they name: `shortlist`: tile t belongs to the device with label index t // 32. One device's 32 tile ids are distinct; at most 8 of them belong to one owner, and in every device exactly 8 belong to some owner. `positives`: every positive label lies in a tile listed by some device of the document's block.
All inputs are finite; a program needn't handle non-finite values.
Results may differ from the reference program's by a relative error of at most 0.0075.
Values may be sent and summed in bfloat16 or wider, within the bound.
No kernel may reach another device: no remote copies, remote signals or barrier semaphores. Data moves between devices by JAX's collectives and lax.ppermute only.
A program may use at most 128 MiB of HBM per device.

```python
import jax
import jax.numpy as jnp
from jax import lax

D = 768
TILE = 64
TILES_DEV = 32
KD = 32
POS = 8
DOC_DEV = 16
C = 8
DOC_BLK = 128
DOCS = 512
TILES = 256
N_LABEL = 8
N_DOC = 4


def listed_tiles(key):
    base = jax.random.fold_in(key, 11)
    keys = jax.random.split(base, N_DOC * N_LABEL)

    def one_device(device_key):
        parts = jax.random.split(device_key, 5)
        first = jax.random.randint(parts[0], (), 0, N_LABEL)
        second = jax.random.randint(parts[1], (), 0, N_LABEL)
        busiest = jnp.minimum(first, second)
        others = (busiest + 1 + jax.random.permutation(parts[2], N_LABEL - 1)) % N_LABEL
        locals_order = jax.random.permutation(parts[3], TILES_DEV)
        positions = jnp.arange(KD, dtype=jnp.int32)
        beyond = jnp.maximum(positions - C, 0)
        cycle = beyond // (N_LABEL - 1)
        owners = jnp.where(positions < C, busiest, others[beyond % (N_LABEL - 1)])
        local_ids = jnp.where(positions < C, locals_order[jnp.minimum(positions, C - 1)], locals_order[C + cycle])
        tile_ids = (owners * TILES_DEV + local_ids).astype(jnp.int32)
        return tile_ids[jax.random.permutation(parts[4], KD)]
    return jax.vmap(one_device)(keys).reshape(N_DOC, N_LABEL, KD)


def owner_directions(key):
    dir_key = jax.random.fold_in(key, 71)
    signs = jax.random.randint(dir_key, (N_LABEL, D), 0, 2).astype(jnp.float32)
    return (2.0 * signs - 1.0) / jnp.sqrt(jnp.float32(D))


def draw_shortlist(key, part):
    return listed_tiles(key)


def draw_positives(key, part):
    lists = listed_tiles(key).reshape(N_DOC, N_LABEL * KD)
    extra = jax.random.fold_in(key, 29)
    first_key, second_key = jax.random.split(extra)
    picks = jax.random.randint(first_key, (DOCS, POS), 0, N_LABEL * KD)
    offsets = jax.random.randint(second_key, (DOCS, POS), 0, TILE)
    block_of = (jnp.arange(DOCS, dtype=jnp.int32) // DOC_BLK)[:, None]
    return (lists[block_of, picks] * TILE + offsets).astype(jnp.int32)


def draw_classifier(key, part):
    directions = owner_directions(key)
    key = jax.random.fold_in(key, 41)
    base = jnp.clip(0.447 * jax.random.normal(key, (TILES, TILE, D), jnp.float32), -2.5, 2.5)
    owner_of = jnp.arange(TILES, dtype=jnp.int32) // TILES_DEV
    values = base + 3.0 * directions[owner_of][:, None, :]
    return values.astype(jnp.bfloat16)


def draw_doc_embed(key, part):
    directions = owner_directions(key)
    key = jax.random.fold_in(key, 53)
    noise_key = jax.random.fold_in(key, 0)
    base = jnp.clip(0.16 * jax.random.normal(noise_key, (DOCS, D), jnp.float32), -0.85, 0.85)
    holder = jnp.arange(DOCS, dtype=jnp.int32) // DOC_DEV % N_LABEL
    values = jnp.clip(base + 0.2 * directions[holder], -1.0, 1.0)
    return values.astype(jnp.bfloat16)


def setup_inputs(seed: int = 0) -> dict:
    arg_keys = jax.random.split(jax.random.key(seed), 5)
    doc_embed = draw_doc_embed(jax.random.fold_in(arg_keys[4], 71), 0)
    classifier = draw_classifier(jax.random.fold_in(arg_keys[4], 71), 0)
    shortlist = draw_shortlist(jax.random.fold_in(arg_keys[4], 71), 0)
    positives = draw_positives(jax.random.fold_in(arg_keys[4], 71), 0)
    return dict(doc_embed=doc_embed, classifier=classifier, shortlist=shortlist, positives=positives)


def reference(doc_embed, classifier, shortlist, positives):
    offsets = jnp.arange(TILE, dtype=jnp.int32)
    start_grad = jnp.zeros(classifier.shape, jnp.float32)
    start_loss = jnp.zeros((), jnp.float32)

    def per_block(carry, block_index):
        class_acc, loss_acc = carry
        doc_panel = lax.dynamic_slice_in_dim(doc_embed, block_index * DOC_BLK, DOC_BLK, 0).astype(jnp.float32)
        wanted = lax.dynamic_slice_in_dim(positives, block_index * DOC_BLK, DOC_BLK, 0)
        lists = lax.dynamic_index_in_dim(shortlist, block_index, 0, keepdims=False)

        def per_list(inner, tile_ids):
            class_in, loss_in, rows_in = inner
            tile_rows = classifier[tile_ids].astype(jnp.float32).reshape(KD * TILE, D)
            label_ids = (tile_ids[:, None] * TILE + offsets[None, :]).reshape(-1)
            scores = jnp.dot(doc_panel, tile_rows.T, precision=lax.Precision.HIGHEST)
            targets = jnp.zeros(scores.shape, scores.dtype)
            for column in range(POS):
                targets = jnp.maximum(targets, (wanted[:, column, None] == label_ids[None, :]).astype(scores.dtype))
            loss_out = loss_in + jnp.sum(jax.nn.softplus(scores) - targets * scores)
            score_grad = ((jax.nn.sigmoid(scores) - targets) * 0.125).astype(jnp.bfloat16)
            score_grad = lax.optimization_barrier(score_grad).astype(jnp.float32)
            rows_out = rows_in + jnp.dot(score_grad, tile_rows, precision=lax.Precision.HIGHEST)
            tile_grad = jnp.dot(score_grad.T, doc_panel, precision=lax.Precision.HIGHEST).astype(jnp.bfloat16)
            tile_grad = lax.optimization_barrier(tile_grad).astype(jnp.float32).reshape(KD, TILE, D)
            class_out = class_in.at[tile_ids].add(tile_grad)
            return (class_out, loss_out, rows_out), None

        rows_start = jnp.zeros((DOC_BLK, D), jnp.float32)
        (class_acc, loss_acc, rows_acc), _ = lax.scan(per_list, (class_acc, loss_acc, rows_start), lists)
        return (class_acc, loss_acc), rows_acc

    (class_grad, loss_sum), row_blocks = lax.scan(per_block, (start_grad, start_loss), jnp.arange(N_DOC, dtype=jnp.int32))
    doc_grad = row_blocks.reshape(DOCS, D).astype(jnp.bfloat16)
    mean_loss = loss_sum / (DOCS * N_LABEL * KD * TILE)
    return doc_grad, class_grad, mean_loss
```

```python
import functools

import jax
import jax.numpy as jnp
from jax import lax
from jax.experimental import pallas as pl
from jax.experimental.pallas import tpu as pltpu
from jax.sharding import PartitionSpec as P

LANES = 128


def flip(size, bit):
    return [(i, i ^ bit) for i in range(size)]


def set_counts(panel, owner, tiles_dev, width, picks):
    rows = panel.shape[0]
    ranks = panel[:, width:].astype(jnp.float32).reshape(rows // 16, 16, LANES)
    flat = jnp.sum(ranks, axis=0)
    first = owner * tiles_dev
    row_ids = lax.broadcasted_iota(jnp.int32, (16, LANES), 0)
    mine = jnp.where(row_ids == first // LANES, flat, 0.0)
    lane_ids = lax.broadcasted_iota(jnp.int32, (LANES, picks.shape[1]), 0)
    spread = (lane_ids == first % LANES + picks).astype(jnp.bfloat16)
    spread_rows = jnp.dot(mine.astype(jnp.bfloat16), spread, preferred_element_type=jnp.float32)
    return jnp.sum(spread_rows, axis=0, keepdims=True)


def score_set(panel, docs, pos_ref, rows, owner, half, core, dims):
    tiles_dev, tile, group, x_half = dims
    labels = rows.shape[0]
    column = lax.broadcasted_iota(jnp.int32, (1, labels), 1)
    slot = column // tile
    local = ((half * x_half + slot // group) * 2 + core) * group + slot % group
    counts = set_counts(panel, owner, tiles_dev, docs.shape[1], local)
    label_ids = (owner * tiles_dev + local) * tile + column % tile
    scores = lax.dot_general(
        docs, rows, (((1,), (1,)), ((), ())), preferred_element_type=jnp.float32
    )
    hit = pos_ref[:, 0:1] == label_ids
    for k in range(1, pos_ref.shape[1]):
        hit = hit | (pos_ref[:, k : k + 1] == label_ids)
    target = hit.astype(jnp.float32)
    small = jnp.exp(-jnp.abs(scores))
    losses = (jnp.maximum(scores, 0.0) + jnp.log1p(small) - target * scores) * counts
    share = 1.0 / (1.0 + small)
    sigmoid = jnp.where(scores >= 0.0, share, small * share)
    weight = ((sigmoid - target) * (counts * 0.125)).astype(jnp.bfloat16)
    return weight, jnp.sum(losses).reshape(1, 1)


def label_grad(weight, docs):
    return lax.dot_general(
        weight, docs, (((0,), (0,)), ((), ())), preferred_element_type=jnp.float32
    )


def first_kernel(dims, width, where_ref, panel_ref, pos_ref, rows_ref, grad_ref, weight_ref, loss_ref):
    panel = panel_ref[...]
    docs = panel[:, :width]
    rows = rows_ref[...].reshape(grad_ref.shape[0], width)
    weight, loss = score_set(
        panel, docs, pos_ref, rows, where_ref[0], where_ref[1], where_ref[2], dims
    )
    grad_ref[...] = label_grad(weight, docs).astype(grad_ref.dtype)
    weight_ref[...] = weight
    loss_ref[...] = loss


def second_kernel(
    dims, width, where_ref, panel_ref, pos_ref, rows_ref, old_rows_ref, old_weight_ref, old_loss_ref,
    grad_ref, part_ref, loss_ref,
):
    panel = panel_ref[...]
    docs = panel[:, :width]
    labels = grad_ref.shape[0]
    rows = rows_ref[...].reshape(labels, width)
    old_rows = old_rows_ref[...].reshape(labels, width)
    weight, loss = score_set(
        panel, docs, pos_ref, rows, where_ref[0], where_ref[1], where_ref[2], dims
    )
    grad_ref[...] = label_grad(weight, docs).astype(grad_ref.dtype)
    part_ref[...] = jnp.dot(weight, rows, preferred_element_type=jnp.float32) + jnp.dot(
        old_weight_ref[...], old_rows, preferred_element_type=jnp.float32
    )
    loss_ref[...] = loss + old_loss_ref[...]


def third_kernel(
    dims, width, where_ref, panel_ref, pos_ref, rows_ref, kept_rows_ref, part_ref, old_loss_ref,
    grad_ref, kept_ref, send_ref,
):
    panel = panel_ref[...]
    docs = panel[:, :width]
    labels = grad_ref.shape[0]
    owner, half, core = where_ref[0], where_ref[1], where_ref[2]
    rows = rows_ref[...].reshape(labels, width)
    weight, loss = score_set(panel, docs, pos_ref, rows, owner, half, core, dims)
    grad_ref[...] = label_grad(weight, docs).astype(grad_ref.dtype)
    part = part_ref[...] + jnp.dot(weight, rows, preferred_element_type=jnp.float32)
    kept_rows = kept_rows_ref[...].reshape(labels, width)
    weight, kept_loss = score_set(panel, docs, pos_ref, kept_rows, owner, half, 1 - core, dims)
    kept_ref[...] = label_grad(weight, docs)
    part = part + jnp.dot(weight, kept_rows, preferred_element_type=jnp.float32)
    send_ref[:, :width] = part.astype(jnp.bfloat16)
    total = loss + kept_loss + old_loss_ref[...]
    top = total.astype(jnp.bfloat16).astype(jnp.float32)
    mid = (total - top).astype(jnp.bfloat16).astype(jnp.float32)
    low = total - top - mid
    lanes = lax.broadcasted_iota(jnp.int32, (send_ref.shape[0], LANES), 1)
    terms = jnp.where(lanes == 0, top, jnp.where(lanes == 1, mid, jnp.where(lanes == 2, low, 0.0)))
    send_ref[:, width:] = terms.astype(jnp.bfloat16)


def per_device(doc_embed, classifier, shortlist, positives):
    label_count = lax.axis_size("label")
    doc_count = lax.axis_size("doc")
    tiles_dev, tile, width = classifier.shape
    doc_dev = doc_embed.shape[0]
    x_count = doc_count // 2
    x_half = x_count // 2
    group = tiles_dev // doc_count
    labels = x_half * group * tile
    block = doc_dev * label_count
    listed = shortlist.size
    owner = lax.axis_index("label")
    place = lax.axis_index("doc")
    core = place % 2
    high = place // 2 // x_half
    dims = (tiles_dev, tile, group, x_half)

    cells = lax.broadcasted_iota(jnp.int32, (16, LANES, listed), 0) * LANES
    cells = cells + lax.broadcasted_iota(jnp.int32, (16, LANES, listed), 1)
    marks = jnp.any(cells == shortlist.reshape(1, 1, listed), axis=2).astype(jnp.bfloat16)
    panel = jnp.concatenate([doc_embed, marks], axis=1)
    bit = 1
    while bit < label_count:
        panel = panel.reshape(1, -1, panel.shape[-1])
        other = lax.ppermute(panel, "label", flip(label_count, bit))
        panel = jnp.concatenate([panel, other], axis=0)
        bit *= 2
    stages = label_count.bit_length() - 1
    panel = panel.reshape((2,) * stages + (doc_dev, width + LANES))
    panel = panel.reshape(block, width + LANES)

    order = lax.iota(jnp.int32, label_count) ^ owner
    wanted = positives.reshape(label_count, doc_dev, positives.shape[1])[order]
    wanted = wanted.reshape(block, positives.shape[1])

    sets = classifier.reshape(2, x_half, 2, group * tile, width)
    full = pl.BlockSpec(memory_space=pltpu.VMEM)

    def rows_spec(swap_half, swap_core):
        def index(i, where):
            half = where[1] if not swap_half else 1 - where[1]
            side = where[2] if not swap_core else 1 - where[2]
            return (half, 0, side, 0, 0)

        return pl.BlockSpec((1, x_half, 1, group * tile, width), index)

    def whole(shape):
        return pl.BlockSpec(shape, lambda i, where: (0,) * len(shape))

    params = pltpu.CompilerParams(vmem_limit_bytes=40 * 1024 * 1024)
    f32, bf16 = jnp.float32, jnp.bfloat16
    shape = jax.ShapeDtypeStruct

    def cost(sets_scored, dots):
        return pl.CostEstimate(
            flops=2 * block * labels * width * dots,
            bytes_accessed=labels * width * 4 * sets_scored,
            transcendentals=3 * block * labels * sets_scored,
        )

    grad_shape = (labels, width)
    panel_spec = whole(panel.shape)
    pos_spec = whole(wanted.shape)
    where = jnp.stack([owner, 1 - high, 1 - core]).astype(jnp.int32)
    grad_a, weight_a, loss_a = pl.pallas_call(
        functools.partial(first_kernel, dims, width),
        grid_spec=pltpu.PrefetchScalarGridSpec(
            num_scalar_prefetch=1,
            grid=(1,),
            in_specs=[panel_spec, pos_spec, rows_spec(False, False)],
            out_specs=[whole(grad_shape), whole((block, labels)), whole((1, 1))],
        ),
        out_shape=[shape(grad_shape, bf16), shape((block, labels), bf16), shape((1, 1), f32)],
        compiler_params=params,
        cost_estimate=cost(1, 2),
    )(where, panel, wanted, sets)
    from_core_a = lax.ppermute(grad_a, "doc", flip(doc_count, 1))

    where = jnp.stack([owner, 1 - high, core]).astype(jnp.int32)
    grad_b, part, loss_b = pl.pallas_call(
        functools.partial(second_kernel, dims, width),
        grid_spec=pltpu.PrefetchScalarGridSpec(
            num_scalar_prefetch=1,
            grid=(1,),
            in_specs=[
                panel_spec, pos_spec, rows_spec(False, False), rows_spec(False, True),
                whole((block, labels)), whole((1, 1)),
            ],
            out_specs=[whole(grad_shape), whole((block, width)), whole((1, 1))],
        ),
        out_shape=[shape(grad_shape, bf16), shape((block, width), f32), shape((1, 1), f32)],
        compiler_params=params,
        cost_estimate=cost(1, 4),
    )(where, panel, wanted, sets, sets, weight_a, loss_a)
    to_x = (grad_b.astype(f32) + from_core_a.astype(f32)).astype(bf16)
    to_x, part = lax.optimization_barrier((to_x, part))
    from_x = lax.ppermute(to_x, "doc", flip(doc_count, doc_count // 2))

    where = jnp.stack([owner, high, 1 - core]).astype(jnp.int32)
    grad_c, kept, send = pl.pallas_call(
        functools.partial(third_kernel, dims, width),
        grid_spec=pltpu.PrefetchScalarGridSpec(
            num_scalar_prefetch=1,
            grid=(1,),
            in_specs=[
                panel_spec, pos_spec, rows_spec(False, False), rows_spec(False, True),
                whole((block, width)), whole((1, 1)),
            ],
            out_specs=[whole(grad_shape), whole(grad_shape), whole((block, width + LANES))],
        ),
        out_shape=[
            shape(grad_shape, bf16), shape(grad_shape, f32), shape((block, width + LANES), bf16)
        ],
        compiler_params=params,
        cost_estimate=cost(2, 6),
    )(where, panel, wanted, sets, sets, part, loss_b)
    from_core_c = lax.ppermute(grad_c, "doc", flip(doc_count, 1))
    kept = kept + from_core_c.astype(f32)

    send = send.reshape(label_count, doc_dev, width + LANES)[order]
    parts = lax.all_to_all(send, "label", split_axis=0, concat_axis=0, tiled=True)
    summed = jnp.sum(parts.astype(f32), axis=0)
    doc_grad = summed[:, :width].astype(bf16)
    loss = jnp.sum(summed[0:1, width : width + 3], axis=1)
    loss = loss + lax.ppermute(loss, "doc", flip(doc_count, 1))
    step = doc_count // 2
    while step > 1:
        loss = loss + lax.ppermute(loss, "doc", flip(doc_count, step))
        step //= 2

    class_grad = kept + from_x.astype(f32)
    class_grad = class_grad.reshape(x_half, group * tile, width)
    step = x_half // 2
    place_x = place // 2
    while step >= 1:
        pairs = class_grad.reshape(2, step, group * tile, width)
        mine = place_x // step % 2
        away = lax.dynamic_index_in_dim(pairs, 1 - mine, 0, keepdims=False)
        stay = lax.dynamic_index_in_dim(pairs, mine, 0, keepdims=False)
        got = lax.ppermute(away.astype(bf16), "doc", flip(doc_count, 2 * step))
        class_grad = stay + got.astype(f32)
        step //= 2
    class_grad = class_grad.reshape(group, tile, width)
    entry_total = block * doc_count * label_count * listed * tile
    return doc_grad, class_grad, loss[0] / entry_total


def solution(mesh):
    placed = (
        P(("doc", "label"), None),
        P("label", None, None),
        P("doc", "label", None),
        P("doc", None),
    )
    return jax.shard_map(
        per_device,
        mesh=mesh,
        in_specs=placed,
        out_specs=(P(("doc", "label"), None), P(("label", "doc"), None, None), P()),
        check_vma=False,
    )
```

```python
import functools

import jax
import jax.numpy as jnp
from jax import lax
from jax.experimental import pallas as pl
from jax.experimental.pallas import tpu as pltpu
from jax.sharding import PartitionSpec as P

LANES = 128
F32, BF16 = jnp.float32, jnp.bfloat16
VMEM = pl.BlockSpec(memory_space=pltpu.VMEM)
HBM = pl.BlockSpec(memory_space=pltpu.HBM)
CHUNKS = 4


def flip(size, bit):
    return [(i, i ^ bit) for i in range(size)]


class Plan:
    def __init__(self, tiles_dev, tile, width, doc_count, label_count, doc_dev):
        self.tiles_dev, self.tile, self.width = tiles_dev, tile, width
        self.x_half = doc_count // 4
        self.group = tiles_dev // doc_count
        self.labels = self.x_half * self.group * tile
        self.block = doc_dev * label_count

    def local_tiles(self, half, core):
        column = lax.broadcasted_iota(jnp.int32, (1, self.labels), 1)
        slot = column // self.tile
        first = (half * self.x_half + slot // self.group) * 2 + core
        return first * self.group + slot % self.group

    def place(self):
        place = lax.axis_index("doc")
        return place // 2 // self.x_half, place % 2

    def order(self, half, core):
        return (1 - half, 1 - core), (1 - half, core), (half, 1 - core), (half, core)

    def rows(self, rows_ref, half, core):
        return rows_ref[half, :, core].reshape(self.labels, self.width)


def ready_kernel(plan, pos_ref, target_ref):
    owner = lax.axis_index("label")
    column = lax.broadcasted_iota(jnp.int32, (1, plan.labels), 1)
    for half in range(2):
        for core in range(2):
            local = plan.local_tiles(half, core)
            label_ids = (owner * plan.tiles_dev + local) * plan.tile + column % plan.tile
            hit = pos_ref[:, 0:1] == label_ids
            for k in range(1, pos_ref.shape[1]):
                hit = hit | (pos_ref[:, k : k + 1] == label_ids)
            target_ref[half, core] = hit.astype(F32).astype(BF16)


def listed_counts(plan, panel_ref):
    marks = panel_ref[:, plan.width :].astype(F32)
    flat = jnp.sum(marks.reshape(plan.block // 16, 16, LANES), axis=0)
    first = lax.axis_index("label") * plan.tiles_dev
    row_ids = lax.broadcasted_iota(jnp.int32, (16, LANES), 0)
    return jnp.where(row_ids == first // LANES, flat, 0.0).astype(BF16)


def set_weights(plan, mine, docs, rows, target, half, core):
    first = lax.axis_index("label") * plan.tiles_dev % LANES
    lane_ids = lax.broadcasted_iota(jnp.int32, (LANES, plan.labels), 0)
    spread = (lane_ids == first + plan.local_tiles(half, core)).astype(F32).astype(BF16)
    counts = jnp.sum(jnp.dot(mine, spread, preferred_element_type=F32), axis=0, keepdims=True)
    scores = lax.dot_general(docs, rows, (((1,), (1,)), ((), ())), preferred_element_type=F32)
    target = target.astype(F32)
    small = jnp.exp(-jnp.abs(scores))
    above = 1.0 + small
    share = 1.0 / above
    log_above = jnp.log(above) + (small - (above - 1.0)) * share
    losses = jnp.maximum(scores, 0.0) + log_above - target * scores
    losses = jnp.sum(losses, axis=0, keepdims=True) * counts
    lane_losses = losses[:, :LANES]
    for start in range(LANES, plan.labels, LANES):
        lane_losses = lane_losses + losses[:, start : start + LANES]
    sigmoid = jnp.where(scores >= 0.0, share, small * share)
    weight = ((sigmoid - target) * (counts * 0.125)).astype(BF16)
    return weight, lane_losses


def label_grad(weight, docs):
    return lax.dot_general(weight, docs, (((0,), (0,)), ((), ())), preferred_element_type=F32)


def first_kernel(plan, panel_ref, rows_ref, target_ref, grad_ref, weight_ref, loss_ref):
    half, core = plan.place()
    docs = panel_ref[:, : plan.width]
    mine = listed_counts(plan, panel_ref)
    losses = jnp.zeros((1, LANES), F32)
    for i, (h, c) in enumerate(plan.order(half, core)):
        weight, more = set_weights(
            plan, mine, docs, plan.rows(rows_ref, h, c), target_ref[h, c], h, c
        )
        weight_ref[i] = weight
        losses = losses + more
        if i == 0:
            grad_ref[...] = label_grad(weight, docs).astype(BF16)
    loss_ref[...] = losses


def second_kernel(plan, panel_ref, weight_ref, core_ref, near_ref, far_ref):
    grad = label_grad(weight_ref[1], panel_ref[:, : plan.width]) + core_ref[...].astype(F32)
    grad = grad.astype(BF16)
    near_ref[...] = grad[: plan.labels // 2]
    far_ref[...] = grad[plan.labels // 2 :]


def third_kernel(
    plan, panel_ref, rows_ref, weight_ref, loss_ref, grad_ref, kept_ref, send_ref
):
    half, core = plan.place()
    docs = panel_ref[:, : plan.width]
    part = jnp.zeros((plan.block, plan.width), F32)
    for i, (h, c) in enumerate(plan.order(half, core)):
        rows = plan.rows(rows_ref, h, c)
        part = part + jnp.dot(weight_ref[i], rows, preferred_element_type=F32)
    send_ref[:, : plan.width] = part.astype(BF16)
    loss = loss_ref[...]
    top = loss.astype(BF16).astype(F32)
    mid = (loss - top).astype(BF16).astype(F32)
    row = lax.broadcasted_iota(jnp.int32, (plan.block, LANES), 0) % 16
    terms = jnp.where(row == 0, top, jnp.where(row == 1, mid, jnp.where(row == 2, loss - top - mid, 0.0)))
    send_ref[:, plan.width :] = terms.astype(BF16)
    grad_ref[...] = label_grad(weight_ref[2], docs).astype(BF16)
    kept_ref[...] = label_grad(weight_ref[3], docs)


def sum_kernel(start, *refs):
    kept_ref, core_ref, x_ref = refs[:3]
    out_hbm, total_ref, sems = refs[-3:]
    count = x_ref.shape[0] // CHUNKS
    copies = []
    for i in range(CHUNKS):
        near, far = pl.ds(i * count, count), pl.ds(start + i * count, count)
        total_ref[near] = kept_ref[far] + core_ref[far].astype(F32) + x_ref[near].astype(F32)
        copy = pltpu.make_async_copy(total_ref.at[near], out_hbm.at[far], sems.at[i])
        copy.start()
        copies.append(copy)
    for copy in copies:
        copy.wait()


def doc_kernel(scale, parts_ref, doc_ref, loss_ref):
    total = jnp.sum(parts_ref[...].astype(F32), axis=0)
    width = doc_ref.shape[1]
    doc_ref[...] = total[:, :width].astype(BF16)
    loss_ref[...] = jnp.full(loss_ref.shape, jnp.sum(total[:, width:]) * scale, F32)


def per_device(doc_embed, classifier, shortlist, positives):
    label_count = lax.axis_size("label")
    doc_count = lax.axis_size("doc")
    tiles_dev, tile, width = classifier.shape
    doc_dev = doc_embed.shape[0]
    plan = Plan(tiles_dev, tile, width, doc_count, label_count, doc_dev)
    block, labels, x_half, group = plan.block, plan.labels, plan.x_half, plan.group
    listed = shortlist.size
    owner = lax.axis_index("label")
    place = lax.axis_index("doc")
    shape = jax.ShapeDtypeStruct
    params = pltpu.CompilerParams(vmem_limit_bytes=16 * 1024 * 1024)

    def cost(dots, scored):
        return pl.CostEstimate(
            flops=2 * block * labels * width * dots,
            bytes_accessed=2 * labels * width * dots,
            transcendentals=3 * block * labels * scored,
        )

    cells = lax.broadcasted_iota(jnp.int32, (16, LANES, listed), 0) * LANES
    cells = cells + lax.broadcasted_iota(jnp.int32, (16, LANES, listed), 1)
    marks = jnp.any(cells == shortlist.reshape(1, 1, listed), axis=2).astype(BF16)
    panel = lax.optimization_barrier(jnp.concatenate([doc_embed, marks], axis=1))
    bit = 1
    while bit < label_count:
        other = lax.ppermute(panel, "label", flip(label_count, bit))
        upper = owner // bit % 2 == 1
        panel = jnp.where(
            upper, jnp.concatenate([other, panel], 0), jnp.concatenate([panel, other], 0)
        )
        if bit == 1:
            early = jnp.abs(panel[0:1, :width]) < jnp.inf
            flat = jnp.where(early, classifier.reshape(-1, width), 0)
        bit *= 2

    rows = flat.reshape(2, x_half, 2, group * tile, width)
    target = pl.pallas_call(
        functools.partial(ready_kernel, plan),
        in_specs=[VMEM],
        out_specs=VMEM,
        out_shape=shape((2, 2, block, labels), BF16),
        compiler_params=params,
        cost_estimate=cost(2, 0),
    )(positives)

    grad_shape = (labels, width)
    grad_a, weights, loss = pl.pallas_call(
        functools.partial(first_kernel, plan),
        in_specs=[VMEM] * 3,
        out_specs=[VMEM] * 3,
        out_shape=[shape(grad_shape, BF16), shape((4, block, labels), BF16), shape((1, LANES), F32)],
        compiler_params=params,
        cost_estimate=cost(5, 4),
    )(panel, rows, target)
    step = doc_count // 2
    from_core_a = lax.ppermute(grad_a, "doc", flip(doc_count, 1))
    half_rows = labels // 2
    grad_c, kept, send = pl.pallas_call(
        functools.partial(third_kernel, plan),
        in_specs=[VMEM] * 4,
        out_specs=[VMEM] * 3,
        out_shape=[
            shape(grad_shape, BF16), shape(grad_shape, F32), shape((block, width + LANES), BF16)
        ],
        compiler_params=params,
        cost_estimate=cost(6, 0),
    )(panel, rows, weights, loss)
    from_core_c = lax.ppermute(grad_c, "doc", flip(doc_count, 1))
    weights, kept, send = lax.optimization_barrier((weights, kept, send))
    to_x = pl.pallas_call(
        functools.partial(second_kernel, plan),
        in_specs=[VMEM] * 3,
        out_specs=[VMEM] * 2,
        out_shape=[shape((half_rows, width), BF16)] * 2,
        compiler_params=params,
        cost_estimate=cost(1, 0),
    )(panel, weights, from_core_a)
    from_x = [lax.ppermute(half, "doc", flip(doc_count, step)) for half in to_x]
    entry_total = block * doc_count * label_count * listed * tile

    def exchange(send):
        send = send.reshape(label_count, doc_dev, width + LANES)
        parts = lax.all_to_all(send, "label", split_axis=0, concat_axis=0, tiled=True)
        doc_grad, loss = pl.pallas_call(
            functools.partial(doc_kernel, 1.0 / entry_total),
            in_specs=[VMEM],
            out_specs=[VMEM, VMEM],
            out_shape=[shape((doc_dev, width), BF16), shape((1, LANES), F32)],
            compiler_params=params,
        )(parts)
        return doc_grad, loss

    def nothing(send):
        return jnp.zeros((doc_dev, width), BF16), jnp.zeros((1, LANES), F32)

    send, *to_x = lax.optimization_barrier((send, *to_x))
    doc_grad, loss = lax.cond(shortlist[0, 0, 0] >= 0, exchange, nothing, send)
    bit = 1
    while bit < doc_count:
        loss = loss + lax.ppermute(loss, "doc", flip(doc_count, bit))
        bit *= 2
    mean_loss = loss[0, 0]

    class_grad = []
    for i in range(2):
        class_grad = [
            pl.pallas_call(
                functools.partial(sum_kernel, i * half_rows),
                in_specs=[VMEM] * 3 + [HBM] * i,
                out_specs=HBM,
                out_shape=shape(grad_shape, F32),
                scratch_shapes=[
                    pltpu.VMEM((half_rows, width), F32), pltpu.SemaphoreType.DMA((CHUNKS,))
                ],
                input_output_aliases={3: 0} if i else {},
                compiler_params=params,
                cost_estimate=cost(1, 0),
            )(kept, from_core_c, from_x[i], *class_grad)
        ]
    class_grad = class_grad[0].reshape(x_half, group * tile, width)
    step = x_half // 2
    while step >= 1:
        pairs = class_grad.reshape(2, step, group * tile, width)
        mine = place // 2 // step % 2
        away = lax.dynamic_index_in_dim(pairs, 1 - mine, 0, keepdims=False)
        stay = lax.dynamic_index_in_dim(pairs, mine, 0, keepdims=False)
        got = lax.ppermute(away.astype(BF16), "doc", flip(doc_count, 2 * step))
        class_grad = stay + got.astype(F32)
        step //= 2
    return doc_grad, class_grad.reshape(group, tile, width), mean_loss


def solution(mesh):
    placed = (
        P(("doc", "label"), None),
        P("label", None, None),
        P("doc", "label", None),
        P("doc", None),
    )
    return jax.shard_map(
        per_device,
        mesh=mesh,
        in_specs=placed,
        out_specs=(P(("doc", "label"), None), P(("label", "doc"), None, None), P()),
        check_vma=False,
    )
```

```python
import functools

import jax
import jax.numpy as jnp
from jax import lax
from jax.experimental import pallas as pl
from jax.experimental.pallas import tpu as pltpu
from jax.sharding import PartitionSpec as P

LANES = 128
F32, BF16 = jnp.float32, jnp.bfloat16
VMEM = pl.BlockSpec(memory_space=pltpu.VMEM)
HBM = pl.BlockSpec(memory_space=pltpu.HBM)
ANY = pl.BlockSpec(memory_space=pl.ANY)
CHUNKS = 4
EXTRA = 16


def flip(size, bit):
    return [(i, i ^ bit) for i in range(size)]


class Plan:
    def __init__(self, tiles_dev, tile, width, doc_count, label_count, doc_dev):
        self.tiles_dev, self.tile, self.width = tiles_dev, tile, width
        self.x_half = doc_count // 4
        self.group = tiles_dev // doc_count
        self.labels = self.x_half * self.group * tile
        self.block = doc_dev * label_count

    def local_tiles(self, half, core):
        column = lax.broadcasted_iota(jnp.int32, (1, self.labels), 1)
        slot = column // self.tile
        first = (half * self.x_half + slot // self.group) * 2 + core
        return first * self.group + slot % self.group

    def place(self):
        place = lax.axis_index("doc")
        return place // 2 // self.x_half, place % 2

    def order(self, half, core):
        return (1 - half, 1 - core), (1 - half, core), (half, 1 - core), (half, core)

    def rows(self, rows_ref, half, core):
        return rows_ref[half, :, core].reshape(self.labels, self.width)


def ready_kernel(plan, pos_ref, target_ref):
    owner = lax.axis_index("label")
    column = lax.broadcasted_iota(jnp.int32, (1, plan.labels), 1)
    for half in range(2):
        for core in range(2):
            local = plan.local_tiles(half, core)
            label_ids = (owner * plan.tiles_dev + local) * plan.tile + column % plan.tile
            hit = pos_ref[:, 0:1] == label_ids
            for k in range(1, pos_ref.shape[1]):
                hit = hit | (pos_ref[:, k : k + 1] == label_ids)
            target_ref[half, core] = hit.astype(F32).astype(BF16)


def listed_counts(plan, panel_ref):
    marks = panel_ref[:, plan.width :].astype(F32)
    flat = jnp.sum(marks.reshape(plan.block // 16, 16, LANES), axis=0)
    first = lax.axis_index("label") * plan.tiles_dev
    row_ids = lax.broadcasted_iota(jnp.int32, (16, LANES), 0)
    return jnp.where(row_ids == first // LANES, flat, 0.0).astype(BF16)


def set_weights(plan, mine, docs, rows, target, half, core):
    first = lax.axis_index("label") * plan.tiles_dev % LANES
    lane_ids = lax.broadcasted_iota(jnp.int32, (LANES, plan.labels), 0)
    spread = (lane_ids == first + plan.local_tiles(half, core)).astype(F32).astype(BF16)
    counts = jnp.sum(jnp.dot(mine, spread, preferred_element_type=F32), axis=0, keepdims=True)
    scores = lax.dot_general(docs, rows, (((1,), (1,)), ((), ())), preferred_element_type=F32)
    target = target.astype(F32)
    small = jnp.exp(-jnp.abs(scores))
    above = 1.0 + small
    share = 1.0 / above
    log_above = jnp.log(above) + (small - (above - 1.0)) * share
    losses = jnp.maximum(scores, 0.0) + log_above - target * scores
    losses = jnp.sum(losses, axis=0, keepdims=True) * counts
    lane_losses = losses[:, :LANES]
    for start in range(LANES, plan.labels, LANES):
        lane_losses = lane_losses + losses[:, start : start + LANES]
    sigmoid = jnp.where(scores >= 0.0, share, small * share)
    weight = ((sigmoid - target) * (counts * 0.125)).astype(BF16)
    return weight, lane_losses


def label_grad(weight, docs):
    return lax.dot_general(weight, docs, (((0,), (0,)), ((), ())), preferred_element_type=F32)


def split_rows(value, count):
    top = value.astype(BF16).astype(F32)
    mid = (value - top).astype(BF16).astype(F32)
    row = lax.broadcasted_iota(jnp.int32, (count, value.shape[1]), 0) % 16
    low = jnp.where(row == 2, value - top - mid, 0.0)
    return jnp.where(row == 0, top, jnp.where(row == 1, mid, low)).astype(BF16)


def first_kernel(plan, panel_ref, rows_ref, target_ref, grad_ref, weight_ref, loss_ref):
    half, core = plan.place()
    docs = panel_ref[:, : plan.width]
    mine = listed_counts(plan, panel_ref)
    losses = jnp.zeros((1, LANES), F32)
    for i, (h, c) in enumerate(plan.order(half, core)):
        weight, more = set_weights(
            plan, mine, docs, plan.rows(rows_ref, h, c), target_ref[h, c], h, c
        )
        weight_ref[i] = weight
        losses = losses + more
        if i == 0:
            grad_ref[: plan.labels] = label_grad(weight, docs).astype(BF16)
    loss_ref[...] = losses
    grad_ref[plan.labels :, :LANES] = split_rows(losses, EXTRA)
    grad_ref[plan.labels :, LANES:] = jnp.zeros((EXTRA, plan.width - LANES), BF16)


def second_kernel(
    plan, panel_ref, weight_ref, core_ref, loss_ref, send_in, near_ref, far_ref, send_ref, terms, sem
):
    theirs = core_ref[plan.labels :, :LANES].astype(F32)
    losses = loss_ref[...] + jnp.sum(theirs, axis=0, keepdims=True)
    terms[...] = split_rows(losses, plan.block)
    copy = pltpu.make_async_copy(terms, send_ref.at[:, pl.ds(plan.width, LANES)], sem)
    copy.start()
    grad = label_grad(weight_ref[1], panel_ref[:, : plan.width])
    grad = (grad + core_ref[: plan.labels].astype(F32)).astype(BF16)
    near = near_ref.shape[0]
    near_ref[...] = grad[:near]
    far_ref[...] = grad[near:]
    copy.wait()


def third_kernel(
    plan, panel_ref, rows_ref, weight_ref, grad_ref, kept_ref, send_ref
):
    half, core = plan.place()
    docs = panel_ref[:, : plan.width]
    part = jnp.zeros((plan.block, plan.width), F32)
    for i, (h, c) in enumerate(plan.order(half, core)):
        rows = plan.rows(rows_ref, h, c)
        part = part + jnp.dot(weight_ref[i], rows, preferred_element_type=F32)
    send_ref[:, : plan.width] = part.astype(BF16)
    send_ref[:, plan.width :] = jnp.zeros((plan.block, LANES), BF16)
    grad_ref[...] = label_grad(weight_ref[2], docs).astype(BF16)
    kept_ref[...] = label_grad(weight_ref[3], docs)


def add_rows(start, kept_ref, core_ref, x_ref, out_hbm, total_ref, sems):
    count = x_ref.shape[0] // CHUNKS
    copies = []
    for i in range(CHUNKS):
        near, far = pl.ds(i * count, count), pl.ds(start + i * count, count)
        total_ref[near] = kept_ref[far] + core_ref[far].astype(F32) + x_ref[near].astype(F32)
        copy = pltpu.make_async_copy(total_ref.at[near], out_hbm.at[far], sems.at[i])
        copy.start()
        copies.append(copy)
    return copies


def near_kernel(kept_ref, core_ref, x_ref, out_hbm, total_ref, sems):
    for copy in add_rows(0, kept_ref, core_ref, x_ref, out_hbm, total_ref, sems):
        copy.wait()


def far_kernel(
    start, kept_ref, core_ref, x_ref, loss_ref, other_ref, out_in, out_hbm, mean_hbm, total_ref, sems,
    mean_ref, mean_sem,
):
    mean_ref[...] = loss_ref[:, :1] + other_ref[:, :1]
    mean_copy = pltpu.make_async_copy(mean_ref, mean_hbm, mean_sem)
    mean_copy.start()
    for copy in add_rows(start, kept_ref, core_ref, x_ref, out_hbm, total_ref, sems):
        copy.wait()
    mean_copy.wait()


def doc_kernel(scale, parts_ref, doc_ref, loss_ref):
    total = jnp.sum(parts_ref[...].astype(F32), axis=0)
    width = doc_ref.shape[1]
    doc_ref[...] = total[:, :width].astype(BF16)
    loss_ref[...] = jnp.full(loss_ref.shape, jnp.sum(total[:, width:]) * scale, F32)


def per_device(doc_embed, classifier, shortlist, positives):
    label_count = lax.axis_size("label")
    doc_count = lax.axis_size("doc")
    tiles_dev, tile, width = classifier.shape
    doc_dev = doc_embed.shape[0]
    plan = Plan(tiles_dev, tile, width, doc_count, label_count, doc_dev)
    block, labels, x_half, group = plan.block, plan.labels, plan.x_half, plan.group
    listed = shortlist.size
    owner = lax.axis_index("label")
    place = lax.axis_index("doc")
    shape = jax.ShapeDtypeStruct
    params = pltpu.CompilerParams(vmem_limit_bytes=8 * 1024 * 1024)

    def cost(dots, scored):
        return pl.CostEstimate(
            flops=2 * block * labels * width * dots,
            bytes_accessed=2 * labels * width * dots,
            transcendentals=3 * block * labels * scored,
        )

    cells = lax.broadcasted_iota(jnp.int32, (16, LANES, listed), 0) * LANES
    cells = cells + lax.broadcasted_iota(jnp.int32, (16, LANES, listed), 1)
    marks = jnp.any(cells == shortlist.reshape(1, 1, listed), axis=2).astype(BF16)
    panel = lax.optimization_barrier(jnp.concatenate([doc_embed, marks], axis=1))
    bit = 1
    while bit < label_count:
        other = lax.ppermute(panel, "label", flip(label_count, bit))
        upper = owner // bit % 2 == 1
        panel = jnp.where(
            upper, jnp.concatenate([other, panel], 0), jnp.concatenate([panel, other], 0)
        )
        if bit == 1:
            early = jnp.abs(panel[0:1, :width]) < jnp.inf
            flat = jnp.where(early, classifier.reshape(-1, width), 0)
        bit *= 2

    rows = flat.reshape(2, x_half, 2, group * tile, width)
    target = pl.pallas_call(
        functools.partial(ready_kernel, plan),
        in_specs=[VMEM],
        out_specs=VMEM,
        out_shape=shape((2, 2, block, labels), BF16),
        compiler_params=params,
        cost_estimate=cost(2, 0),
    )(positives)

    grad_shape = (labels, width)
    grad_a, weights, loss = pl.pallas_call(
        functools.partial(first_kernel, plan),
        in_specs=[VMEM] * 3,
        out_specs=[VMEM] * 3,
        out_shape=[
            shape((labels + EXTRA, width), BF16), shape((4, block, labels), BF16), shape((1, LANES), F32)
        ],
        compiler_params=params,
        cost_estimate=cost(5, 4),
    )(panel, rows, target)
    step = doc_count // 2
    from_core_a = lax.ppermute(grad_a, "doc", flip(doc_count, 1))
    near = labels * 3 // 4
    grad_c, kept, send = pl.pallas_call(
        functools.partial(third_kernel, plan),
        in_specs=[VMEM] * 3,
        out_specs=[VMEM] * 3,
        out_shape=[
            shape(grad_shape, BF16), shape(grad_shape, F32), shape((block, width + LANES), BF16)
        ],
        compiler_params=params,
        cost_estimate=cost(6, 0),
    )(panel, rows, weights)
    from_core_c = lax.ppermute(grad_c, "doc", flip(doc_count, 1))
    weights, kept, send = lax.optimization_barrier((weights, kept, send))
    *to_x, send = pl.pallas_call(
        functools.partial(second_kernel, plan),
        in_specs=[VMEM] * 4 + [ANY],
        out_specs=[VMEM] * 2 + [ANY],
        out_shape=[
            shape((near, width), BF16), shape((labels - near, width), BF16), shape(send.shape, BF16)
        ],
        scratch_shapes=[pltpu.VMEM((block, LANES), BF16), pltpu.SemaphoreType.DMA(())],
        input_output_aliases={4: 2},
        compiler_params=params,
        cost_estimate=cost(1, 0),
    )(panel, weights, from_core_a, loss, send)
    from_x = [lax.ppermute(half, "doc", flip(doc_count, step)) for half in to_x]
    entry_total = block * doc_count * label_count * listed * tile

    def exchange(send):
        send = send.reshape(label_count, doc_dev, width + LANES)
        parts = lax.all_to_all(send, "label", split_axis=0, concat_axis=0, tiled=True)
        doc_grad, loss = pl.pallas_call(
            functools.partial(doc_kernel, 1.0 / entry_total),
            in_specs=[VMEM],
            out_specs=[VMEM, VMEM],
            out_shape=[shape((doc_dev, width), BF16), shape((1, LANES), F32)],
            compiler_params=params,
        )(parts)
        return doc_grad, loss

    def nothing(send):
        return jnp.zeros((doc_dev, width), BF16), jnp.zeros((1, LANES), F32)

    send, *to_x = lax.optimization_barrier((send, *to_x))
    doc_grad, loss = lax.cond(shortlist[0, 0, 0] >= 0, exchange, nothing, send)
    bit, other = 2, jnp.zeros((1, LANES), F32)
    while bit < doc_count:
        loss = loss + other if bit > 2 else loss
        other = lax.ppermute(loss, "doc", flip(doc_count, bit))
        bit *= 2

    def scratch(count):
        return [pltpu.VMEM((count, width), F32), pltpu.SemaphoreType.DMA((CHUNKS,))]

    class_grad = pl.pallas_call(
        near_kernel,
        in_specs=[VMEM] * 3,
        out_specs=HBM,
        out_shape=shape(grad_shape, F32),
        scratch_shapes=scratch(near),
        compiler_params=params,
        cost_estimate=cost(1, 0),
    )(kept, from_core_c, from_x[0])
    class_grad, mean_loss = pl.pallas_call(
        functools.partial(far_kernel, near),
        in_specs=[VMEM] * 5 + [HBM],
        out_specs=[HBM, HBM],
        out_shape=[shape(grad_shape, F32), shape((1, 1), F32)],
        scratch_shapes=scratch(labels - near)
        + [pltpu.VMEM((1, 1), F32), pltpu.SemaphoreType.DMA(())],
        input_output_aliases={5: 0},
        compiler_params=params,
        cost_estimate=cost(1, 0),
    )(kept, from_core_c, from_x[1], loss, other, class_grad)
    mean_loss = mean_loss.reshape(())
    class_grad = class_grad.reshape(x_half, group * tile, width)
    step = x_half // 2
    while step >= 1:
        pairs = class_grad.reshape(2, step, group * tile, width)
        mine = place // 2 // step % 2
        away = lax.dynamic_index_in_dim(pairs, 1 - mine, 0, keepdims=False)
        stay = lax.dynamic_index_in_dim(pairs, mine, 0, keepdims=False)
        got = lax.ppermute(away.astype(BF16), "doc", flip(doc_count, 2 * step))
        class_grad = stay + got.astype(F32)
        step //= 2
    return doc_grad, class_grad.reshape(group, tile, width), mean_loss


def solution(mesh):
    placed = (
        P(("doc", "label"), None),
        P("label", None, None),
        P("doc", "label", None),
        P("doc", None),
    )
    return jax.shard_map(
        per_device,
        mesh=mesh,
        in_specs=placed,
        out_specs=(P(("doc", "label"), None), P(("label", "doc"), None, None), P()),
        check_vma=False,
    )
```

```python
import functools

import jax
import jax.numpy as jnp
from jax import lax
from jax.experimental import pallas as pl
from jax.experimental.pallas import tpu as pltpu
from jax.sharding import PartitionSpec as P

LANES = 128
EXTRA = 16
F32, BF16 = jnp.float32, jnp.bfloat16
VMEM = pl.BlockSpec(memory_space=pltpu.VMEM)
HBM = pl.BlockSpec(memory_space=pltpu.HBM)


def flip(size, bit):
    return [(i, i ^ bit) for i in range(size)]


class Plan:
    def __init__(self, tiles_dev, tile, width, doc_count, label_count, doc_dev):
        self.tiles_dev, self.tile, self.width = tiles_dev, tile, width
        self.x_half = doc_count // 4
        self.group = tiles_dev // doc_count
        self.labels = self.x_half * self.group * tile
        self.block = doc_dev * label_count

    def local_tiles(self, half, core):
        column = lax.broadcasted_iota(jnp.int32, (1, self.labels), 1)
        slot = column // self.tile
        first = (half * self.x_half + slot // self.group) * 2 + core
        return first * self.group + slot % self.group

    def place(self):
        place = lax.axis_index("doc")
        return place // 2 // self.x_half, place % 2

    def order(self, half, core):
        return (1 - half, 1 - core), (1 - half, core), (half, 1 - core), (half, core)

    def rows(self, rows_ref, half, core):
        return rows_ref[half, :, core].reshape(self.labels, self.width)


def ready_kernel(plan, pos_ref, target_ref):
    owner = lax.axis_index("label")
    column = lax.broadcasted_iota(jnp.int32, (1, plan.labels), 1)
    for half in range(2):
        for core in range(2):
            local = plan.local_tiles(half, core)
            label_ids = (owner * plan.tiles_dev + local) * plan.tile + column % plan.tile
            hit = pos_ref[:, 0:1] == label_ids
            for k in range(1, pos_ref.shape[1]):
                hit = hit | (pos_ref[:, k : k + 1] == label_ids)
            target_ref[half, core] = hit.astype(F32).astype(BF16)


def listed_counts(plan, panel_ref):
    marks = panel_ref[:, plan.width :].astype(F32)
    flat = jnp.sum(marks.reshape(plan.block // 16, 16, LANES), axis=0)
    first = lax.axis_index("label") * plan.tiles_dev
    row_ids = lax.broadcasted_iota(jnp.int32, (16, LANES), 0)
    return jnp.where(row_ids == first // LANES, flat, 0.0).astype(BF16)


def set_weights(plan, mine, docs, rows, target, half, core):
    first = lax.axis_index("label") * plan.tiles_dev % LANES
    lane_ids = lax.broadcasted_iota(jnp.int32, (LANES, plan.labels), 0)
    spread = (lane_ids == first + plan.local_tiles(half, core)).astype(F32).astype(BF16)
    counts = jnp.sum(jnp.dot(mine, spread, preferred_element_type=F32), axis=0, keepdims=True)
    scores = lax.dot_general(docs, rows, (((1,), (1,)), ((), ())), preferred_element_type=F32)
    target = target.astype(F32)
    small = jnp.exp(-jnp.abs(scores))
    above = 1.0 + small
    share = 1.0 / above
    log_above = jnp.log(above) + (small - (above - 1.0)) * share
    losses = jnp.maximum(scores, 0.0) + log_above - target * scores
    losses = jnp.sum(losses, axis=0, keepdims=True) * counts
    lane_losses = losses[:, :LANES]
    for start in range(LANES, plan.labels, LANES):
        lane_losses = lane_losses + losses[:, start : start + LANES]
    sigmoid = jnp.where(scores >= 0.0, share, small * share)
    weight = ((sigmoid - target) * (counts * 0.125)).astype(BF16)
    return weight, lane_losses


def label_grad(weight, docs):
    return lax.dot_general(weight, docs, (((0,), (0,)), ((), ())), preferred_element_type=F32)


def split_rows(value, count):
    top = value.astype(BF16).astype(F32)
    mid = (value - top).astype(BF16).astype(F32)
    row = lax.broadcasted_iota(jnp.int32, (count, value.shape[1]), 0) % 16
    low = jnp.where(row == 2, value - top - mid, 0.0)
    return jnp.where(row == 0, top, jnp.where(row == 1, mid, low)).astype(BF16)


def first_kernel(plan, panel_ref, rows_ref, target_ref, far_ref, near_ref, loss_ref):
    half, core = plan.place()
    docs = panel_ref[:, : plan.width]
    mine = listed_counts(plan, panel_ref)
    losses = jnp.zeros(loss_ref.shape, F32)
    for i, (h, c) in enumerate(plan.order(half, core)):
        weight, more = set_weights(
            plan, mine, docs, plan.rows(rows_ref, h, c), target_ref[h, c], h, c
        )
        if i < 2:
            far_ref[i] = weight
        else:
            near_ref[(i - 2) * plan.block : (i - 1) * plan.block] = weight
        losses = losses + more
    loss_ref[...] = losses
    near_ref[2 * plan.block :, :LANES] = split_rows(losses, EXTRA)
    near_ref[2 * plan.block :, LANES:] = jnp.zeros((EXTRA, plan.labels - LANES), BF16)


def send_kernel(plan, far_ref, near_ref, rows_ref, loss_ref, core_ref, send_ref):
    half, core = plan.place()
    part = jnp.zeros((plan.block, plan.width), F32)
    for i, (h, c) in enumerate(plan.order(half, core)):
        weight = far_ref[i] if i < 2 else near_ref[(i - 2) * plan.block : (i - 1) * plan.block]
        part = part + jnp.dot(weight, plan.rows(rows_ref, h, c), preferred_element_type=F32)
    send_ref[:, : plan.width] = part.astype(BF16)
    theirs = core_ref[2 * plan.block :, :LANES].astype(F32)
    losses = loss_ref[...] + jnp.sum(theirs, axis=0, keepdims=True)
    send_ref[:, plan.width :] = split_rows(losses, plan.block)


def last_kernel(
    plan, panel_ref, near_ref, panel_c_ref, near_c_ref, panel_x_ref, far_x_ref, panel_xc_ref,
    far_xc_ref, out_hbm, sum_ref, sems,
):
    copies = []
    for start in range(0, plan.labels, LANES):
        part = pl.ds(start, LANES)
        sum_ref[part] = (
            label_grad(near_ref[pl.ds(plan.block, plan.block), part], panel_ref[:, : plan.width])
            + label_grad(near_c_ref[pl.ds(0, plan.block), part], panel_c_ref[:, : plan.width])
            + label_grad(far_x_ref[1, :, part], panel_x_ref[:, : plan.width])
            + label_grad(far_xc_ref[0, :, part], panel_xc_ref[:, : plan.width])
        )
        copies.append(
            pltpu.make_async_copy(sum_ref.at[part], out_hbm.at[part], sems.at[len(copies)])
        )
        copies[-1].start()
    for copy in copies:
        copy.wait()


def doc_kernel(scale, parts_ref, doc_ref, loss_ref):
    total = jnp.sum(parts_ref[...].astype(F32), axis=0)
    width = doc_ref.shape[1]
    doc_ref[...] = total[:, :width].astype(BF16)
    loss_ref[...] = jnp.full(loss_ref.shape, jnp.sum(total[:, width:]) * scale, F32)


def per_device(doc_embed, classifier, shortlist, positives):
    label_count = lax.axis_size("label")
    doc_count = lax.axis_size("doc")
    tiles_dev, tile, width = classifier.shape
    doc_dev = doc_embed.shape[0]
    plan = Plan(tiles_dev, tile, width, doc_count, label_count, doc_dev)
    block, labels, x_half, group = plan.block, plan.labels, plan.x_half, plan.group
    listed = shortlist.size
    owner = lax.axis_index("label")
    place = lax.axis_index("doc")
    shape = jax.ShapeDtypeStruct
    params = pltpu.CompilerParams(vmem_limit_bytes=8 * 1024 * 1024)

    def cost(dots, scored):
        return pl.CostEstimate(
            flops=2 * block * labels * width * dots,
            bytes_accessed=2 * labels * width * dots,
            transcendentals=3 * block * labels * scored,
        )

    cells = lax.broadcasted_iota(jnp.int32, (16, LANES, listed), 0) * LANES
    cells = cells + lax.broadcasted_iota(jnp.int32, (16, LANES, listed), 1)
    marks = jnp.any(cells == shortlist.reshape(1, 1, listed), axis=2).astype(BF16)
    panel = lax.optimization_barrier(jnp.concatenate([doc_embed, marks], axis=1))
    bit = 1
    while bit < label_count:
        other = lax.ppermute(panel, "label", flip(label_count, bit))
        upper = owner // bit % 2 == 1
        panel = jnp.where(
            upper, jnp.concatenate([other, panel], 0), jnp.concatenate([panel, other], 0)
        )
        if bit == 1:
            early = jnp.abs(panel[0:1, :width]) < jnp.inf
            flat = jnp.where(early, classifier.reshape(-1, width), 0)
        bit *= 2

    rows = flat.reshape(2, x_half, 2, group * tile, width)
    target = pl.pallas_call(
        functools.partial(ready_kernel, plan),
        in_specs=[VMEM],
        out_specs=VMEM,
        out_shape=shape((2, 2, block, labels), BF16),
        compiler_params=params,
        cost_estimate=cost(2, 0),
    )(positives)

    grad_shape, pair_shape = (labels, width), (2, block, labels)

    def kernel(body, count, outs, dots, scored=0, **options):
        return pl.pallas_call(
            functools.partial(body, plan),
            in_specs=[VMEM] * count,
            out_specs=options.pop("out_specs", [VMEM] * len(outs)),
            out_shape=outs,
            compiler_params=params,
            cost_estimate=cost(dots, scored),
            **options,
        )

    near_shape = (2 * block + EXTRA, labels)
    far, near, loss = kernel(
        first_kernel, 3, [shape(pair_shape, BF16), shape(near_shape, BF16), shape((1, LANES), F32)],
        4, 4,
    )(panel, rows, target)
    step = doc_count // 2
    near_c = lax.ppermute(near, "doc", flip(doc_count, 1))
    panel_c = lax.ppermute(panel, "doc", flip(doc_count, 1))
    far_x = lax.ppermute(far, "doc", flip(doc_count, step))
    panel_x = lax.ppermute(panel, "doc", flip(doc_count, step))
    (send,) = kernel(send_kernel, 5, [shape((block, width + LANES), BF16)], 4)(
        far, near, rows, loss, near_c
    )
    send = send.reshape(label_count, doc_dev, width + LANES)
    parts = lax.all_to_all(send, "label", split_axis=0, concat_axis=0, tiled=True)

    far_xc = lax.ppermute(far_x, "doc", flip(doc_count, 1))
    panel_xc = lax.ppermute(panel_x, "doc", flip(doc_count, 1))
    class_grad = kernel(
        last_kernel, 8, shape(grad_shape, F32), 4,
        out_specs=HBM,
        scratch_shapes=[
            pltpu.VMEM(grad_shape, F32), pltpu.SemaphoreType.DMA((labels // LANES,))
        ],
    )(panel, near, panel_c, near_c, panel_x, far_x, panel_xc, far_xc)

    parts, class_grad = lax.optimization_barrier((parts, class_grad))
    entry_total = block * doc_count * label_count * listed * tile
    doc_grad, loss = pl.pallas_call(
        functools.partial(doc_kernel, 1.0 / entry_total),
        in_specs=[VMEM],
        out_specs=[VMEM, VMEM],
        out_shape=[shape((doc_dev, width), BF16), shape((1, LANES), F32)],
        compiler_params=params,
    )(parts)
    bit, other = 2, jnp.zeros((1, LANES), F32)
    while bit < doc_count:
        loss = loss + other if bit > 2 else loss
        other = lax.ppermute(loss, "doc", flip(doc_count, bit))
        bit *= 2
    mean_loss = (loss + other)[0, 0]
    class_grad = class_grad.reshape(x_half, group * tile, width)
    step = x_half // 2
    while step >= 1:
        pairs = class_grad.reshape(2, step, group * tile, width)
        mine = place // 2 // step % 2
        away = lax.dynamic_index_in_dim(pairs, 1 - mine, 0, keepdims=False)
        stay = lax.dynamic_index_in_dim(pairs, mine, 0, keepdims=False)
        got = lax.ppermute(away.astype(BF16), "doc", flip(doc_count, 2 * step))
        class_grad = stay + got.astype(F32)
        step //= 2
    return doc_grad, class_grad.reshape(group, tile, width), mean_loss


def solution(mesh):
    placed = (
        P(("doc", "label"), None),
        P("label", None, None),
        P("doc", "label", None),
        P("doc", None),
    )
    return jax.shard_map(
        per_device,
        mesh=mesh,
        in_specs=placed,
        out_specs=(P(("doc", "label"), None), P(("label", "doc"), None, None), P()),
        check_vma=False,
    )
```

```python
import functools

import jax
import jax.numpy as jnp
from jax import lax
from jax.experimental import pallas as pl
from jax.experimental.pallas import tpu as pltpu
from jax.sharding import PartitionSpec as P

LANES = 128
EXTRA = 16
F32, BF16 = jnp.float32, jnp.bfloat16
VMEM = pl.BlockSpec(memory_space=pltpu.VMEM)
HBM = pl.BlockSpec(memory_space=pltpu.HBM)


def flip(size, bit):
    return [(i, i ^ bit) for i in range(size)]


class Plan:
    def __init__(self, tiles_dev, tile, width, doc_count, label_count, doc_dev):
        self.tiles_dev, self.tile, self.width = tiles_dev, tile, width
        self.x_half = doc_count // 4
        self.group = tiles_dev // doc_count
        self.labels = self.x_half * self.group * tile
        self.block = doc_dev * label_count

    def local_tiles(self, half, core):
        column = lax.broadcasted_iota(jnp.int32, (1, self.labels), 1)
        slot = column // self.tile
        first = (half * self.x_half + slot // self.group) * 2 + core
        return first * self.group + slot % self.group

    def place(self):
        place = lax.axis_index("doc")
        return place // 2 // self.x_half, place % 2

    def order(self, half, core):
        return (1 - half, 1 - core), (1 - half, core), (half, 1 - core), (half, core)

    def rows(self, rows_ref, half, core):
        return rows_ref[half, :, core].reshape(self.labels, self.width)


def ready_kernel(plan, pos_ref, target_ref):
    owner = lax.axis_index("label")
    column = lax.broadcasted_iota(jnp.int32, (1, plan.labels), 1)
    for half in range(2):
        for core in range(2):
            local = plan.local_tiles(half, core)
            label_ids = (owner * plan.tiles_dev + local) * plan.tile + column % plan.tile
            hit = pos_ref[:, 0:1] == label_ids
            for k in range(1, pos_ref.shape[1]):
                hit = hit | (pos_ref[:, k : k + 1] == label_ids)
            target_ref[half, core] = hit.astype(F32).astype(BF16)


def listed_counts(plan, panel_ref):
    marks = panel_ref[:, plan.width :].astype(F32)
    flat = jnp.sum(marks.reshape(plan.block // 16, 16, LANES), axis=0)
    first = lax.axis_index("label") * plan.tiles_dev
    row_ids = lax.broadcasted_iota(jnp.int32, (16, LANES), 0)
    return jnp.where(row_ids == first // LANES, flat, 0.0).astype(BF16)


def set_weights(plan, mine, docs, rows, target, half, core):
    first = lax.axis_index("label") * plan.tiles_dev % LANES
    lane_ids = lax.broadcasted_iota(jnp.int32, (LANES, plan.labels), 0)
    spread = (lane_ids == first + plan.local_tiles(half, core)).astype(F32).astype(BF16)
    counts = jnp.sum(jnp.dot(mine, spread, preferred_element_type=F32), axis=0, keepdims=True)
    scores = lax.dot_general(docs, rows, (((1,), (1,)), ((), ())), preferred_element_type=F32)
    target = target.astype(F32)
    small = jnp.exp(-jnp.abs(scores))
    above = 1.0 + small
    share = 1.0 / above
    log_above = jnp.log(above) + (small - (above - 1.0)) * share
    losses = jnp.maximum(scores, 0.0) + log_above - target * scores
    losses = jnp.sum(losses, axis=0, keepdims=True) * counts
    lane_losses = losses[:, :LANES]
    for start in range(LANES, plan.labels, LANES):
        lane_losses = lane_losses + losses[:, start : start + LANES]
    sigmoid = jnp.where(scores >= 0.0, share, small * share)
    weight = ((sigmoid - target) * (counts * 0.125)).astype(BF16)
    return weight, lane_losses


def label_grad(weight, docs):
    return lax.dot_general(weight, docs, (((0,), (0,)), ((), ())), preferred_element_type=F32)


def split_rows(value, count):
    top = value.astype(BF16).astype(F32)
    mid = (value - top).astype(BF16).astype(F32)
    row = lax.broadcasted_iota(jnp.int32, (count, value.shape[1]), 0) % 16
    low = jnp.where(row == 2, value - top - mid, 0.0)
    return jnp.where(row == 0, top, jnp.where(row == 1, mid, low)).astype(BF16)


def first_kernel(plan, panel_ref, rows_ref, target_ref, far_ref, near_ref, loss_ref):
    half, core = plan.place()
    docs = panel_ref[:, : plan.width]
    mine = listed_counts(plan, panel_ref)
    losses = jnp.zeros(loss_ref.shape, F32)
    for i, (h, c) in enumerate(plan.order(half, core)):
        weight, more = set_weights(
            plan, mine, docs, plan.rows(rows_ref, h, c), target_ref[h, c], h, c
        )
        if i < 2:
            far_ref[i] = weight
        else:
            near_ref[(i - 2) * plan.block : (i - 1) * plan.block] = weight
        losses = losses + more
    loss_ref[...] = losses
    near_ref[2 * plan.block :, :LANES] = split_rows(losses, EXTRA)
    near_ref[2 * plan.block :, LANES:] = jnp.zeros((EXTRA, plan.labels - LANES), BF16)


def send_kernel(plan, far_ref, near_ref, rows_ref, loss_ref, core_ref, send_ref):
    half, core = plan.place()
    part = jnp.zeros((plan.block, plan.width), F32)
    for i, (h, c) in enumerate(plan.order(half, core)):
        weight = far_ref[i] if i < 2 else near_ref[(i - 2) * plan.block : (i - 1) * plan.block]
        part = part + jnp.dot(weight, plan.rows(rows_ref, h, c), preferred_element_type=F32)
    send_ref[:, : plan.width] = part.astype(BF16)
    theirs = core_ref[2 * plan.block :, :LANES].astype(F32)
    losses = loss_ref[...] + jnp.sum(theirs, axis=0, keepdims=True)
    send_ref[:, plan.width :] = split_rows(losses, plan.block)


def last_kernel(
    plan, panel_ref, near_ref, panel_c_ref, near_c_ref, panel_x_ref, far_x_ref, panel_xc_ref,
    far_xc_ref, out_hbm, sum_ref, sems,
):
    copies = []
    for start in range(0, plan.labels, LANES):
        part = pl.ds(start, LANES)
        sum_ref[part] = (
            label_grad(near_ref[pl.ds(plan.block, plan.block), part], panel_ref[:, : plan.width])
            + label_grad(near_c_ref[pl.ds(0, plan.block), part], panel_c_ref[:, : plan.width])
            + label_grad(far_x_ref[1, :, part], panel_x_ref[:, : plan.width])
            + label_grad(far_xc_ref[0, :, part], panel_xc_ref[:, : plan.width])
        )
        copies.append(
            pltpu.make_async_copy(sum_ref.at[part], out_hbm.at[part], sems.at[len(copies)])
        )
        copies[-1].start()
    for copy in copies:
        copy.wait()


def doc_kernel(parts_ref, doc_ref):
    width = doc_ref.shape[1]
    doc_ref[...] = jnp.sum(parts_ref[:, :, :width].astype(F32), axis=0).astype(BF16)


def loss_kernel(scale, parts_ref, loss_ref):
    total = jnp.sum(parts_ref[:, :, parts_ref.shape[2] - LANES :].astype(F32), axis=0)
    loss_ref[...] = jnp.full(loss_ref.shape, jnp.sum(total) * scale, F32)


def per_device(doc_embed, classifier, shortlist, positives):
    label_count = lax.axis_size("label")
    doc_count = lax.axis_size("doc")
    tiles_dev, tile, width = classifier.shape
    doc_dev = doc_embed.shape[0]
    plan = Plan(tiles_dev, tile, width, doc_count, label_count, doc_dev)
    block, labels, x_half, group = plan.block, plan.labels, plan.x_half, plan.group
    listed = shortlist.size
    owner = lax.axis_index("label")
    place = lax.axis_index("doc")
    shape = jax.ShapeDtypeStruct
    params = pltpu.CompilerParams(vmem_limit_bytes=8 * 1024 * 1024)

    def cost(dots, scored):
        return pl.CostEstimate(
            flops=2 * block * labels * width * dots,
            bytes_accessed=2 * labels * width * dots,
            transcendentals=3 * block * labels * scored,
        )

    cells = lax.broadcasted_iota(jnp.int32, (16, LANES, listed), 0) * LANES
    cells = cells + lax.broadcasted_iota(jnp.int32, (16, LANES, listed), 1)
    marks = jnp.any(cells == shortlist.reshape(1, 1, listed), axis=2).astype(BF16)
    panel = lax.optimization_barrier(jnp.concatenate([doc_embed, marks], axis=1))
    bit = 1
    while bit < label_count:
        other = lax.ppermute(panel, "label", flip(label_count, bit))
        upper = owner // bit % 2 == 1
        panel = jnp.where(
            upper, jnp.concatenate([other, panel], 0), jnp.concatenate([panel, other], 0)
        )
        if bit == 1:
            early = jnp.abs(panel[0:1, :width]) < jnp.inf
            flat = jnp.where(early, classifier.reshape(-1, width), 0)
        bit *= 2

    rows = flat.reshape(2, x_half, 2, group * tile, width)
    target = pl.pallas_call(
        functools.partial(ready_kernel, plan),
        in_specs=[VMEM],
        out_specs=VMEM,
        out_shape=shape((2, 2, block, labels), BF16),
        compiler_params=params,
        cost_estimate=cost(2, 0),
    )(positives)

    grad_shape, pair_shape = (labels, width), (2, block, labels)

    def kernel(body, count, outs, dots, scored=0, **options):
        return pl.pallas_call(
            functools.partial(body, plan),
            in_specs=[VMEM] * count,
            out_specs=options.pop("out_specs", [VMEM] * len(outs)),
            out_shape=outs,
            compiler_params=params,
            cost_estimate=cost(dots, scored),
            **options,
        )

    near_shape = (2 * block + EXTRA, labels)
    far, near, loss = kernel(
        first_kernel, 3, [shape(pair_shape, BF16), shape(near_shape, BF16), shape((1, LANES), F32)],
        4, 4,
    )(panel, rows, target)
    step = doc_count // 2
    near_c = lax.ppermute(near, "doc", flip(doc_count, 1))
    panel_c = lax.ppermute(panel, "doc", flip(doc_count, 1))
    far_x = lax.ppermute(far, "doc", flip(doc_count, step))
    panel_x = lax.ppermute(panel, "doc", flip(doc_count, step))
    (send,) = kernel(send_kernel, 5, [shape((block, width + LANES), BF16)], 4)(
        far, near, rows, loss, near_c
    )
    send = send.reshape(label_count, doc_dev, width + LANES)
    parts = lax.all_to_all(send, "label", split_axis=0, concat_axis=0, tiled=True)

    far_xc = lax.ppermute(far_x, "doc", flip(doc_count, 1))
    panel_xc = lax.ppermute(panel_x, "doc", flip(doc_count, 1))
    class_grad = kernel(
        last_kernel, 8, shape(grad_shape, F32), 4,
        out_specs=HBM,
        scratch_shapes=[
            pltpu.VMEM(grad_shape, F32), pltpu.SemaphoreType.DMA((labels // LANES,))
        ],
    )(panel, near, panel_c, near_c, panel_x, far_x, panel_xc, far_xc)

    parts, class_grad = lax.optimization_barrier((parts, class_grad))
    entry_total = block * doc_count * label_count * listed * tile
    loss = pl.pallas_call(
        functools.partial(loss_kernel, 1.0 / entry_total),
        in_specs=[VMEM],
        out_specs=VMEM,
        out_shape=shape((1, LANES), F32),
        compiler_params=params,
    )(parts)
    bit, other = 2, jnp.zeros((1, LANES), F32)
    while bit < doc_count:
        loss = loss + other if bit > 2 else loss
        other = lax.ppermute(loss, "doc", flip(doc_count, bit))
        bit *= 2
    doc_grad = pl.pallas_call(
        doc_kernel,
        in_specs=[VMEM],
        out_specs=VMEM,
        out_shape=shape((doc_dev, width), BF16),
        compiler_params=params,
    )(parts)
    doc_grad, other = lax.optimization_barrier((doc_grad, other))
    mean_loss = (loss + other)[0, 0]
    class_grad = class_grad.reshape(x_half, group * tile, width)
    step = x_half // 2
    while step >= 1:
        pairs = class_grad.reshape(2, step, group * tile, width)
        mine = place // 2 // step % 2
        away = lax.dynamic_index_in_dim(pairs, 1 - mine, 0, keepdims=False)
        stay = lax.dynamic_index_in_dim(pairs, mine, 0, keepdims=False)
        got = lax.ppermute(away.astype(BF16), "doc", flip(doc_count, 2 * step))
        class_grad = stay + got.astype(F32)
        step //= 2
    return doc_grad, class_grad.reshape(group, tile, width), mean_loss


def solution(mesh):
    placed = (
        P(("doc", "label"), None),
        P("label", None, None),
        P("doc", "label", None),
        P("doc", None),
    )
    return jax.shard_map(
        per_device,
        mesh=mesh,
        in_specs=placed,
        out_specs=(P(("doc", "label"), None), P(("label", "doc"), None, None), P()),
        check_vma=False,
    )
```

```python
import functools

import jax
import jax.numpy as jnp
from jax import lax
from jax.experimental import pallas as pl
from jax.experimental.pallas import tpu as pltpu
from jax.sharding import PartitionSpec as P

LANES = 128
EXTRA = 48
F32, BF16 = jnp.float32, jnp.bfloat16
VMEM = pl.BlockSpec(memory_space=pltpu.VMEM)
HBM = pl.BlockSpec(memory_space=pltpu.HBM)


def flip(size, bit):
    return [(i, i ^ bit) for i in range(size)]


class Plan:
    def __init__(self, tiles_dev, tile, width, doc_count, label_count, doc_dev):
        self.tiles_dev, self.tile, self.width = tiles_dev, tile, width
        self.x_half = doc_count // 4
        self.group = tiles_dev // doc_count
        self.labels = self.x_half * self.group * tile
        self.block = doc_dev * label_count

    def local_tiles(self, half, core):
        column = lax.broadcasted_iota(jnp.int32, (1, self.labels), 1)
        slot = column // self.tile
        first = (half * self.x_half + slot // self.group) * 2 + core
        return first * self.group + slot % self.group

    def place(self):
        place = lax.axis_index("doc")
        return place // 2 // self.x_half, place % 2

    def order(self, half, core):
        return (1 - half, 1 - core), (1 - half, core), (half, 1 - core), (half, core)

    def rows(self, rows_ref, half, core):
        return rows_ref[half, :, core].reshape(self.labels, self.width)


def ready_kernel(plan, pos_ref, target_ref):
    owner = lax.axis_index("label")
    column = lax.broadcasted_iota(jnp.int32, (1, plan.labels), 1)
    for half in range(2):
        for core in range(2):
            local = plan.local_tiles(half, core)
            label_ids = (owner * plan.tiles_dev + local) * plan.tile + column % plan.tile
            hit = pos_ref[:, 0:1] == label_ids
            for k in range(1, pos_ref.shape[1]):
                hit = hit | (pos_ref[:, k : k + 1] == label_ids)
            target_ref[half, core] = hit.astype(F32).astype(BF16)


def listed_counts(plan, panel_ref):
    marks = panel_ref[:, plan.width :].astype(F32)
    flat = jnp.sum(marks.reshape(plan.block // 16, 16, LANES), axis=0)
    first = lax.axis_index("label") * plan.tiles_dev
    row_ids = lax.broadcasted_iota(jnp.int32, (16, LANES), 0)
    return jnp.where(row_ids == first // LANES, flat, 0.0).astype(BF16)


def set_weights(plan, mine, docs, rows, target, half, core):
    first = lax.axis_index("label") * plan.tiles_dev % LANES
    lane_ids = lax.broadcasted_iota(jnp.int32, (LANES, plan.labels), 0)
    spread = (lane_ids == first + plan.local_tiles(half, core)).astype(F32).astype(BF16)
    counts = jnp.sum(jnp.dot(mine, spread, preferred_element_type=F32), axis=0, keepdims=True)
    scores = lax.dot_general(docs, rows, (((1,), (1,)), ((), ())), preferred_element_type=F32)
    target = target.astype(F32)
    small = jnp.exp(-jnp.abs(scores))
    above = 1.0 + small
    share = 1.0 / above
    log_above = jnp.log(above) + (small - (above - 1.0)) * share
    losses = jnp.maximum(scores, 0.0) + log_above - target * scores
    losses = jnp.sum(losses, axis=0, keepdims=True) * counts
    lane_losses = losses[:, :LANES]
    for start in range(LANES, plan.labels, LANES):
        lane_losses = lane_losses + losses[:, start : start + LANES]
    sigmoid = jnp.where(scores >= 0.0, share, small * share)
    weight = ((sigmoid - target) * (counts * 0.125)).astype(BF16)
    return weight, lane_losses


def label_grad(weight, docs):
    return lax.dot_general(weight, docs, (((0,), (0,)), ((), ())), preferred_element_type=F32)


def split_rows(value, count):
    top = value.astype(BF16).astype(F32)
    mid = (value - top).astype(BF16).astype(F32)
    row = lax.broadcasted_iota(jnp.int32, (count, value.shape[1]), 0) % 16
    low = jnp.where(row == 2, value - top - mid, 0.0)
    return jnp.where(row == 0, top, jnp.where(row == 1, mid, low)).astype(BF16)


def first_kernel(
    plan, panel_ref, rows_ref, target_ref, far_ref, near_ref, own_ref, loss_ref
):
    half, core = plan.place()
    width, labels, block = plan.width, plan.labels, plan.block
    docs = panel_ref[:, :width]
    mine = listed_counts(plan, panel_ref)
    losses = jnp.zeros(loss_ref.shape, F32)
    far_ref[:, :width] = docs
    near_ref[:block, :width] = docs
    for i, (h, c) in enumerate(plan.order(half, core)):
        weight, more = set_weights(
            plan, mine, docs, plan.rows(rows_ref, h, c), target_ref[h, c], h, c
        )
        if i < 2:
            far_ref[:, width + i * labels : width + (i + 1) * labels] = weight
        elif i == 2:
            near_ref[:block, width:] = weight
        else:
            own_ref[...] = weight
        losses = losses + more
    loss_ref[...] = losses
    near_ref[block:, :LANES] = split_rows(losses, EXTRA)
    near_ref[block:, LANES:] = jnp.zeros((EXTRA, width + labels - LANES), BF16)


def send_kernel(plan, far_ref, near_ref, own_ref, rows_ref, loss_ref, core_ref, send_ref):
    half, core = plan.place()
    width, labels, block = plan.width, plan.labels, plan.block
    part = jnp.zeros((block, width), F32)
    for i, (h, c) in enumerate(plan.order(half, core)):
        if i < 2:
            weight = far_ref[:, width + i * labels : width + (i + 1) * labels]
        else:
            weight = near_ref[:block, width:] if i == 2 else own_ref[...]
        part = part + jnp.dot(weight, plan.rows(rows_ref, h, c), preferred_element_type=F32)
    send_ref[:, :, :width] = part.astype(BF16).reshape(block // 16, 16, width)
    theirs = core_ref[block : block + 16, :LANES].astype(F32)
    losses = loss_ref[...] + jnp.sum(theirs, axis=0, keepdims=True)
    send_ref[:, :, width:] = split_rows(losses, block).reshape(block // 16, 16, LANES)


def last_kernel(
    plan, panel_ref, own_ref, core_ref, x_ref, xc_ref, parts_ref, out_hbm, doc_hbm,
    sum_ref, doc_ref, sems,
):
    width, labels, block = plan.width, plan.labels, plan.block
    doc_ref[...] = jnp.sum(parts_ref[:, :, :width].astype(F32), axis=0).astype(BF16)
    copies = [pltpu.make_async_copy(doc_ref, doc_hbm, sems.at[0])]
    copies[0].start()
    for start in range(0, labels, LANES):
        first, second = width + start, width + labels + start
        part = pl.ds(start, LANES)
        sum_ref[part] = (
            label_grad(own_ref[:, start : start + LANES], panel_ref[:, :width])
            + label_grad(core_ref[:block, first : first + LANES], core_ref[:block, :width])
            + label_grad(x_ref[:, second : second + LANES], x_ref[:, :width])
            + label_grad(xc_ref[:, first : first + LANES], xc_ref[:, :width])
        )
        copies.append(
            pltpu.make_async_copy(sum_ref.at[part], out_hbm.at[part], sems.at[len(copies)])
        )
        copies[-1].start()
    for copy in copies:
        copy.wait()


def loss_kernel(scale, parts_ref, loss_ref):
    total = jnp.sum(parts_ref[:, :, parts_ref.shape[2] - LANES :].astype(F32), axis=0)
    loss_ref[...] = jnp.full(loss_ref.shape, jnp.sum(total) * scale, F32)


def per_device(doc_embed, classifier, shortlist, positives):
    label_count = lax.axis_size("label")
    doc_count = lax.axis_size("doc")
    tiles_dev, tile, width = classifier.shape
    doc_dev = doc_embed.shape[0]
    plan = Plan(tiles_dev, tile, width, doc_count, label_count, doc_dev)
    block, labels, x_half, group = plan.block, plan.labels, plan.x_half, plan.group
    listed = shortlist.size
    owner = lax.axis_index("label")
    place = lax.axis_index("doc")
    shape = jax.ShapeDtypeStruct
    params = pltpu.CompilerParams(vmem_limit_bytes=8 * 1024 * 1024)

    def cost(dots, scored):
        return pl.CostEstimate(
            flops=2 * block * labels * width * dots,
            bytes_accessed=2 * labels * width * dots,
            transcendentals=3 * block * labels * scored,
        )

    cells = lax.broadcasted_iota(jnp.int32, (16, LANES, listed), 0) * LANES
    cells = cells + lax.broadcasted_iota(jnp.int32, (16, LANES, listed), 1)
    marks = jnp.any(cells == shortlist.reshape(1, 1, listed), axis=2).astype(BF16)
    panel = lax.optimization_barrier(jnp.concatenate([doc_embed, marks], axis=1))
    bit = 1
    while bit < label_count:
        other = lax.ppermute(panel, "label", flip(label_count, bit))
        upper = owner // bit % 2 == 1
        panel = jnp.where(
            upper, jnp.concatenate([other, panel], 0), jnp.concatenate([panel, other], 0)
        )
        if bit == 1:
            early = jnp.abs(panel[0:1, :width]) < jnp.inf
            flat = jnp.where(early, classifier.reshape(-1, width), 0)
        bit *= 2

    rows = flat.reshape(2, x_half, 2, group * tile, width)
    target = pl.pallas_call(
        functools.partial(ready_kernel, plan),
        in_specs=[VMEM],
        out_specs=VMEM,
        out_shape=shape((2, 2, block, labels), BF16),
        compiler_params=params,
        cost_estimate=cost(2, 0),
    )(positives)

    grad_shape = (labels, width)

    def kernel(body, count, outs, dots, scored=0, **options):
        return pl.pallas_call(
            functools.partial(body, plan),
            in_specs=[VMEM] * count,
            out_specs=options.pop("out_specs", [VMEM] * len(outs)),
            out_shape=outs,
            compiler_params=params,
            cost_estimate=cost(dots, scored),
            **options,
        )

    far, near, own, loss = kernel(
        first_kernel, 3,
        [
            shape((block, width + 2 * labels), BF16), shape((block + EXTRA, width + labels), BF16),
            shape((block, labels), BF16), shape((1, LANES), F32),
        ],
        4, 4,
    )(panel, rows, target)
    step = doc_count // 2
    from_core = lax.ppermute(near, "doc", flip(doc_count, 1))
    from_x = lax.ppermute(far, "doc", flip(doc_count, step))
    (send,) = kernel(send_kernel, 6, [shape((label_count, doc_dev, width + LANES), BF16)], 4)(
        far, near, own, rows, loss, from_core
    )

    def exchange(send):
        return lax.all_to_all(send, "label", split_axis=0, concat_axis=0, tiled=True)

    parts = lax.cond(shortlist[0, 0, 0] >= 0, exchange, jnp.zeros_like, send)
    parts, from_x = lax.optimization_barrier((parts, from_x))
    over_core = lax.ppermute(from_x, "doc", flip(doc_count, 1))
    class_grad, doc_grad = kernel(
        last_kernel, 6, [shape(grad_shape, F32), shape((doc_dev, width), BF16)], 4,
        out_specs=[HBM, HBM],
        scratch_shapes=[
            pltpu.VMEM(grad_shape, F32), pltpu.VMEM((doc_dev, width), BF16),
            pltpu.SemaphoreType.DMA((labels // LANES + 1,)),
        ],
    )(panel, own, from_core, from_x, over_core, parts)

    entry_total = block * doc_count * label_count * listed * tile
    loss = pl.pallas_call(
        functools.partial(loss_kernel, 1.0 / entry_total),
        in_specs=[VMEM],
        out_specs=VMEM,
        out_shape=shape((1, LANES), F32),
        compiler_params=params,
    )(parts)
    bit, other = 2, jnp.zeros((1, LANES), F32)
    while bit < doc_count:
        loss = loss + other if bit > 2 else loss
        other = lax.ppermute(loss, "doc", flip(doc_count, bit))
        bit *= 2
    class_grad, other = lax.optimization_barrier((class_grad, other))
    mean_loss = (loss + other)[0, 0]
    class_grad = class_grad.reshape(x_half, group * tile, width)
    step = x_half // 2
    while step >= 1:
        pairs = class_grad.reshape(2, step, group * tile, width)
        mine = place // 2 // step % 2
        away = lax.dynamic_index_in_dim(pairs, 1 - mine, 0, keepdims=False)
        stay = lax.dynamic_index_in_dim(pairs, mine, 0, keepdims=False)
        got = lax.ppermute(away.astype(BF16), "doc", flip(doc_count, 2 * step))
        class_grad = stay + got.astype(F32)
        step //= 2
    return doc_grad, class_grad.reshape(group, tile, width), mean_loss


def solution(mesh):
    placed = (
        P(("doc", "label"), None),
        P("label", None, None),
        P("doc", "label", None),
        P("doc", None),
    )
    return jax.shard_map(
        per_device,
        mesh=mesh,
        in_specs=placed,
        out_specs=(P(("doc", "label"), None), P(("label", "doc"), None, None), P()),
        check_vma=False,
    )
```
